32 devices in a mesh: groups: 2 (over y), tensor: 4 (over z), dp: 4 (over x, core).
Axes of the slice: x: 2, y: 2, z: 4, core: 2. Of those that a mesh axis runs over, the one named last changes fastest.
Arguments:
- inputs: bfloat16 [1024, 8192], P(('groups', 'dp', 'tensor')), parts along dimension 0, may hold values from -6 to 6
- grad_out: bfloat16 [1024, 8192], P(('groups', 'dp', 'tensor')), parts along dimension 0, may hold values from -40 to 40
- w_gate: bfloat16 [8192, 14336], P('dp', 'tensor'), may hold values from -0.0625 to 0.0625
- w_up: bfloat16 [8192, 14336], P('dp', 'tensor'), may hold values from -0.0625 to 0.0625
- w_down: bfloat16 [14336, 8192], P('tensor', 'dp'), may hold values from -0.046875 to 0.046875
- proj_input: bfloat16 [8192, 32], replicated, may hold values from -0.0625 to 0.0625
- proj_gate: bfloat16 [14336, 32], P('tensor'), may hold values from -0.046875 to 0.046875
- proj_up: bfloat16 [14336, 32], P('tensor'), may hold values from -0.046875 to 0.046875
- proj_hidden: bfloat16 [14336, 32], P('tensor'), may hold values from -0.046875 to 0.046875
- proj_out: bfloat16 [8192, 32], replicated, may hold values from -0.0625 to 0.0625
- example_ids: int32 [8, 128], P(('groups', 'dp')), parts along dimension 0, may hold values from 0 to 3, never falling along the last dimension, each value on 1 to 64 neighbouring positions
Outputs:
- d_input: bfloat16 [1024, 8192], P(('groups', 'dp', 'tensor')), parts along dimension 0
- grads: float32 [3, 32, 1024], P(None, ('groups', 'dp')), parts along dimension 1
- fisher: float32 [6, 2, 1024], P('groups'), parts along dimension 0
The draws below stay inside these ranges and needn't reach their ends.
There are 2 independent parts, one for each index of `groups`. The reference program is written for one: setup_inputs(seed, part) draws one part's arguments, and reference() takes and returns one part's arrays. A program takes and returns all parts, laid end to end along the dimension named above; an argument that names none is the same for every part. Nothing has to cross between parts.
Inputs may be any that keep to these rules, and one draw needn't show every extreme that they name: `example_ids`: along each row the ids never fall; each of the 4 examples of a row holds 1 to 64 tokens, and one of them exactly 64.
All inputs are finite; a program needn't handle non-finite values.
Results may differ from the reference program's by a relative error of at most 0.0049.
Values may be sent and summed in bfloat16 or wider, within the bound.
A program may use at most 448 MiB of HBM per device.

```python
import math
import jax
import jax.numpy as jnp
import numpy as np
from jax import lax

D = 8192
FFW = 14336
R = 32
MOST = 64
TOK_DP = 128
EX_DP = 4
TOKENS = 512
EXAMPLES = 16
N_DP = 4


def draw_grad_out(key, part):
    key = jax.random.fold_in(key, 7)
    key_base, key_rows, key_cols = jax.random.split(key, 3)
    positions = jnp.arange(TOKENS, dtype=jnp.float32) / TOKENS
    rise = (3.0 ** positions)[:, None]
    rough = jnp.exp(jax.random.uniform(key_rows, (TOKENS, 1), jnp.float32, 0.0, math.log(4.0)))
    column = jnp.exp(jax.random.uniform(key_cols, (1, D), jnp.float32, -math.log(2.0), math.log(2.0)))
    base = jax.random.normal(key_base, (TOKENS, D), jnp.float32)
    base = jnp.clip(base, -4.0, 4.0)
    return (0.4 * rise * rough * column * base).astype(jnp.bfloat16)


def block_scale(key, extent, cuts, low, top_value):
    def one(axis_at, parts):
        heights = jax.random.uniform(jax.random.fold_in(jax.random.fold_in(key, 6), axis_at), (parts,), jnp.float32, low / len(cuts), top_value / len(cuts))
        return jnp.repeat(jnp.exp(heights), extent[axis_at] // parts).reshape((-1,) + (1,) * (len(extent) - axis_at - 1))

    gain = one(*cuts[0])
    for cut in cuts[1:]:
        gain = gain * one(*cut)
    return gain


def profile(amount, total, bound, lean):
    loads = [(1 << 20) // math.isqrt(rank ** lean) + 1 for rank in range(2, amount + 1)]
    rest, given = total - bound - (amount - 1), [1] * (amount - 1)
    while rest > 0:
        movable = [i for i in range(amount - 1) if given[i] < bound]
        whole, budget = sum([loads[i] for i in movable]), rest
        for i in movable:
            addition = min(bound - given[i], max(1, budget * loads[i] // whole), rest)
            given[i] = given[i] + addition
            rest = rest - addition
    return np.array([bound] + given)


def uneven(rng, count, total, reach, lean):
    if count == 2:
        one = jax.random.randint(rng, (), max(1, total - reach), min(reach, total - 1) + 1)
        return jnp.stack([one, total - one])
    sizes = jnp.asarray(profile(count, total, reach, lean), jnp.int32)
    couples = (count - 1) // 2
    donor, sink = sizes[1:1 + 2 * couples:2], sizes[2:2 + 2 * couples:2]
    room = jnp.minimum(donor - 1, reach - sink)
    moved = jax.random.randint(jax.random.fold_in(rng, 1), (couples,), 0, 1 << 20) % (room + 1)
    sizes = sizes.at[1:1 + 2 * couples:2].set(donor - moved).at[2:2 + 2 * couples:2].set(sink + moved)
    return sizes[jax.random.permutation(jax.random.fold_in(rng, 2), count)]


def normal_values(own_key, dims, spread, bound, cuts=(), held_as=jnp.bfloat16):
    values = jax.random.normal(own_key, dims, jnp.float32) * spread
    if len(cuts) > 0:
        values = block_scale(own_key, dims, cuts, -0.22, 0.18) * values
    return jnp.clip(values, min=-bound, max=bound).astype(held_as)


def setup_inputs(seed: int = 0, part: int = 0) -> dict:
    key_of = jax.random.split(jax.random.key(seed), 12)
    part_keys = jax.random.split(jax.random.fold_in(key_of[11], part), 12)
    inputs = normal_values(part_keys[0], (TOKENS, D), 1.0, 6.0, ((0, 16),))
    grad_out = draw_grad_out(jax.random.fold_in(jax.random.fold_in(key_of[11], part), 71), part)
    w_gate = normal_values(key_of[2], (D, FFW), D ** -0.5, 0.0625, ((0, 4), (1, 4)))
    w_up = normal_values(key_of[3], (D, FFW), D ** -0.5, 0.0625, ((0, 4), (1, 4)))
    w_down = normal_values(key_of[4], (FFW, D), FFW ** -0.5, 0.046875, ((0, 4), (1, 4)))
    proj_input = normal_values(key_of[5], (D, R), D ** -0.5, 0.0625)
    proj_gate = normal_values(key_of[6], (FFW, R), FFW ** -0.5, 0.046875, ((0, 4),))
    proj_up = normal_values(key_of[7], (FFW, R), FFW ** -0.5, 0.046875, ((0, 4),))
    proj_hidden = normal_values(key_of[8], (FFW, R), FFW ** -0.5, 0.046875, ((0, 4),))
    proj_out = normal_values(key_of[9], (D, R), D ** -0.5, 0.0625)
    example_ids = jax.vmap(lambda own: jnp.searchsorted(jnp.cumsum(uneven(own, EX_DP, TOK_DP, MOST, 0)), jnp.arange(TOK_DP), side="right"))(jax.random.split(part_keys[10], N_DP)).reshape((N_DP, TOK_DP)).astype(jnp.int32)
    return {"inputs": inputs, "grad_out": grad_out, "w_gate": w_gate, "w_up": w_up, "w_down": w_down, "proj_input": proj_input, "proj_gate": proj_gate, "proj_up": proj_up, "proj_hidden": proj_hidden, "proj_out": proj_out, "example_ids": example_ids}


def example_grads(onehot, left, right):
    return 0.125 * jnp.einsum("et,ti,tj->eij", onehot, left, right, precision=lax.Precision.HIGHEST)


def reference(inputs, grad_out, w_gate, w_up, w_down, proj_input, proj_gate, proj_up, proj_hidden, proj_out, example_ids):
    contract = (((1,), (1,)), ((), ()))
    gate = jnp.dot(inputs, w_gate, preferred_element_type=jnp.float32)
    upper = jnp.dot(inputs, w_up, preferred_element_type=jnp.float32)
    sigma = jax.nn.sigmoid(gate)
    active = gate * sigma
    hidden = (active * upper).astype(jnp.bfloat16)
    hidden_grad = lax.dot_general(grad_out, w_down, contract, preferred_element_type=jnp.float32)
    upper_grad = (hidden_grad * active).astype(jnp.bfloat16)
    gate_grad = (hidden_grad * upper * sigma * (1.0 + gate * (1.0 - sigma))).astype(jnp.bfloat16)
    d_input = (lax.dot_general(gate_grad, w_gate, contract, preferred_element_type=jnp.float32)
               + lax.dot_general(upper_grad, w_up, contract, preferred_element_type=jnp.float32)).astype(jnp.bfloat16)
    input_proj = jnp.dot(inputs, proj_input, preferred_element_type=jnp.float32)
    out_proj = jnp.dot(grad_out, proj_out, preferred_element_type=jnp.float32)
    hidden_proj = jnp.dot(hidden, proj_hidden, preferred_element_type=jnp.float32)
    gate_proj = jnp.dot(gate_grad, proj_gate, preferred_element_type=jnp.float32)
    up_proj = jnp.dot(upper_grad, proj_up, preferred_element_type=jnp.float32)
    offsets = (jnp.arange(N_DP, dtype=jnp.int32) * EX_DP).astype(jnp.int32)
    global_ids = (example_ids + offsets[:, None]).reshape(-1)
    numbers = jnp.arange(EXAMPLES, dtype=jnp.int32)
    onehot = (global_ids[None, :] == numbers[:, None]).astype(jnp.float32)
    stacked = jnp.stack([example_grads(onehot, input_proj, gate_proj),
                         example_grads(onehot, input_proj, up_proj),
                         example_grads(onehot, hidden_proj, out_proj)])
    grads = stacked.reshape(3, EXAMPLES, R * R)
    left_side = jnp.einsum("meik,mejk->mij", stacked, stacked, precision=lax.Precision.HIGHEST)
    right_side = jnp.einsum("meki,mekj->mij", stacked, stacked, precision=lax.Precision.HIGHEST)
    fisher = (jnp.stack([left_side, right_side], axis=1) / EXAMPLES).reshape(3, 2, R * R)
    return d_input, grads, fisher
```

```python
import jax
import jax.numpy as jnp
from jax import lax
from jax.sharding import PartitionSpec as P

R = 32
EX_DP = 4
PARTS = 2


def example_grads(onehot, left, right):
    return 0.125 * jnp.einsum("et,ti,tj->eij", onehot, left, right, precision=lax.Precision.HIGHEST)


def swap(value, bit, size):
    return lax.ppermute(value, "dp", [(i, i ^ bit) for i in range(size)])


def per_device(
    inputs,
    grad_out,
    w_gate,
    w_up,
    w_down,
    proj_input,
    proj_gate,
    proj_up,
    proj_hidden,
    proj_out,
    example_ids,
):
    contract = (((1,), (1,)), ((), ()))
    f32, bf16 = jnp.float32, jnp.bfloat16
    dp_size = lax.axis_size("dp")
    tensor_size = lax.axis_size("tensor")
    me = lax.axis_index("dp")
    rows, width = inputs.shape
    depth, units = w_gate.shape
    parts = min(PARTS, rows)
    step = rows // parts
    tokens = tensor_size * step

    order = (0, 2, 1, 3)

    def columns(value):
        blocks = value.reshape(rows, dp_size, depth)
        slots = []
        for b in order:
            block = lax.dynamic_index_in_dim(blocks, me ^ b, 1, keepdims=False)
            slots.append(block if b == 0 else swap(block, b, dp_size))
        return jnp.stack(slots)

    in_cols, cot_cols = columns(inputs), columns(grad_out)
    in_own = jnp.dot(inputs, proj_input, preferred_element_type=f32)
    out_own = jnp.dot(grad_out, proj_out, preferred_element_type=f32)
    own_proj = lax.all_gather(jnp.stack([in_own, out_own]), "tensor", axis=1, tiled=True)

    def gathered(value, k):
        own = value[:, k * step : (k + 1) * step]
        full = lax.all_gather(own, "tensor", axis=1, tiled=True)
        return full.reshape(dp_size * tokens, depth)

    def summed(part):
        part = part.reshape(2, 2 * tokens, units)
        half = part[0] + swap(part[1], 1, dp_size)
        half = half.reshape(2, tokens, units)
        return half[0] + swap(half[1].astype(bf16), 2, dp_size).astype(f32)

    def spread(value):
        pair = jnp.concatenate([value, swap(value, 2, dp_size)])
        return jnp.concatenate([pair, swap(pair, 1, dp_size)])

    projected, returned = [], []
    for k in range(parts):
        x = gathered(in_cols, k)
        gate = summed(jnp.dot(x, w_gate, preferred_element_type=f32))
        upper = summed(jnp.dot(x, w_up, preferred_element_type=f32))
        g = gathered(cot_cols, k)
        hidden_grad = summed(lax.dot_general(g, w_down, contract, preferred_element_type=f32))
        sigma = jax.nn.sigmoid(gate)
        active = gate * sigma
        hidden = (active * upper).astype(bf16)
        upper_grad = (hidden_grad * active).astype(bf16)
        gate_grad = (hidden_grad * upper * sigma * (1.0 + gate * (1.0 - sigma))).astype(bf16)
        projected.append(
            jnp.stack(
                [
                    jnp.dot(gate_grad, proj_gate, preferred_element_type=f32),
                    jnp.dot(upper_grad, proj_up, preferred_element_type=f32),
                    jnp.dot(hidden, proj_hidden, preferred_element_type=f32),
                ]
            ).reshape(3, tensor_size, step, R)
        )
        d_part = lax.dot_general(spread(gate_grad), w_gate, contract, preferred_element_type=f32)
        d_part += lax.dot_general(spread(upper_grad), w_up, contract, preferred_element_type=f32)
        d_part = d_part.reshape(dp_size, tokens, depth)
        d_own = lax.psum_scatter(d_part, "tensor", scatter_dimension=1, tiled=True).astype(bf16)
        slots = []
        for at, b in enumerate(order):
            slots.append(d_own[at] if b == 0 else swap(d_own[at], b, dp_size))
        returned.append(jnp.stack(slots))

    where = jnp.array([order.index(b) for b in range(dp_size)], jnp.int32)[jnp.arange(dp_size) ^ me]
    d_slots = jnp.concatenate(returned, axis=1)
    d_input = jnp.take(d_slots, where, axis=0).transpose(1, 0, 2).reshape(rows, width)

    projections = jnp.stack(projected, axis=2).reshape(3, tensor_size * rows, R)
    gate_proj, up_proj, hidden_proj = lax.psum(projections, "tensor")
    input_proj, out_proj = own_proj
    local_ids = example_ids[0]
    numbers = lax.broadcasted_iota(jnp.int32, (EX_DP, tensor_size * rows), 0)
    onehot = (local_ids[None, :] == numbers).astype(f32)
    stacked = jnp.stack(
        [
            example_grads(onehot, input_proj, gate_proj),
            example_grads(onehot, input_proj, up_proj),
            example_grads(onehot, hidden_proj, out_proj),
        ]
    )
    grads = stacked.reshape(3, EX_DP, R * R)
    left_side = jnp.einsum("meik,mejk->mij", stacked, stacked, precision=lax.Precision.HIGHEST)
    right_side = jnp.einsum("meki,mekj->mij", stacked, stacked, precision=lax.Precision.HIGHEST)
    total = lax.psum(jnp.stack([left_side, right_side], axis=1), "dp")
    fisher = (total / (EX_DP * dp_size)).reshape(3, 2, R * R)
    return (d_input, grads, fisher)


def solution(mesh):
    return jax.shard_map(
        per_device,
        mesh=mesh,
        in_specs=(
            P(("groups", "dp", "tensor"), None),
            P(("groups", "dp", "tensor"), None),
            P("dp", "tensor"),
            P("dp", "tensor"),
            P("tensor", "dp"),
            P(),
            P("tensor", None),
            P("tensor", None),
            P("tensor", None),
            P(),
            P(("groups", "dp"), None),
        ),
        out_specs=(
            P(("groups", "dp", "tensor"), None),
            P(None, ("groups", "dp"), None),
            P("groups", None, None),
        ),
        check_vma=False,
    )
```

```python
import jax
import jax.numpy as jnp
from jax import lax
from jax.sharding import PartitionSpec as P

R = 32
EX_DP = 4
PARTS = 2
ORDER = (0, 2, 1, 3)
CONTRACT = (((1,), (1,)), ((), ()))
f32, bf16 = jnp.float32, jnp.bfloat16


def example_grads(onehot, left, right):
    return 0.125 * jnp.einsum("et,ti,tj->eij", onehot, left, right, precision=lax.Precision.HIGHEST)


def swap(value, bit, axis="dp"):
    return lax.ppermute(value, axis, [(i, i ^ bit) for i in range(lax.axis_size(axis))])


def after(value, *others):
    return lax.optimization_barrier((value,) + others)[0]


def columns(value, depth):
    me = lax.axis_index("dp")
    rows = value.shape[0]
    slots = []
    for b in ORDER:
        block = lax.dynamic_slice(value, (0, (me ^ b) * depth), (rows, depth))
        slots.append(block if b == 0 else swap(block, b))
    return jnp.stack(slots)


def uncolumns(slots):
    me = lax.axis_index("dp")
    count, rows, depth = slots.shape
    came = [slots[at] if b == 0 else swap(slots[at], b) for at, b in enumerate(ORDER)]
    where = jnp.array([ORDER.index(b) for b in range(count)], jnp.int32)[jnp.arange(count) ^ me]
    return jnp.take(jnp.stack(came), where, axis=0).transpose(1, 0, 2).reshape(rows, count * depth)


def halved(part):
    part = part.reshape(2, part.shape[0] // 2, part.shape[1])
    return part[0] + swap(part[1], 1)


def finished(half):
    half = half.reshape(2, half.shape[0] // 2, half.shape[1])
    return half[0] + swap(half[1].astype(bf16), 2).astype(f32)


def spread(value):
    pair = jnp.concatenate([value, swap(value, 2)])
    return jnp.concatenate([pair, swap(pair, 1)])


def partials(x, g, w_gate, w_up, w_down):
    return (
        jnp.dot(x, w_gate, preferred_element_type=f32),
        jnp.dot(x, w_up, preferred_element_type=f32),
        lax.dot_general(g, w_down, CONTRACT, preferred_element_type=f32),
    )


def middle(gate, upper, hidden_grad):
    sigma = jax.nn.sigmoid(gate)
    active = gate * sigma
    hidden = (active * upper).astype(bf16)
    upper_grad = (hidden_grad * active).astype(bf16)
    gate_grad = (hidden_grad * upper * sigma * (1.0 + gate * (1.0 - sigma))).astype(bf16)
    return hidden, gate_grad, upper_grad


def project(hidden, gate_grad, upper_grad, proj_gate, proj_up, proj_hidden):
    return jnp.stack(
        [
            jnp.dot(gate_grad, proj_gate, preferred_element_type=f32),
            jnp.dot(upper_grad, proj_up, preferred_element_type=f32),
            jnp.dot(hidden, proj_hidden, preferred_element_type=f32),
        ]
    )


def back(gate_grad, upper_grad, w_gate, w_up):
    part = lax.dot_general(spread(gate_grad), w_gate, CONTRACT, preferred_element_type=f32)
    return part + lax.dot_general(spread(upper_grad), w_up, CONTRACT, preferred_element_type=f32)


def line(own):
    me = lax.axis_index("tensor")
    left = [own]
    right = [own]
    for s in range(1, 4):
        left.append(lax.ppermute(left[-1], "tensor", [(t, t + 1) for t in range(s - 1, 3)]))
        right.append(lax.ppermute(right[-1], "tensor", [(t + 1, t) for t in range(0, 4 - s)]))
    second = jnp.where(me % 2 == 0, right[1], left[1])
    third = jnp.where(me < 2, right[2], left[2])
    near = jnp.where(me == 1, right[1], left[1])
    far = jnp.where(me == 0, right[3], left[3])
    return own, second, third, jnp.where((me == 0) | (me == 3), far, near)


def four(inputs, grad_out, w_gate, w_up, w_down, proj_input, proj_gate, proj_up, proj_hidden, proj_out):
    me = lax.axis_index("tensor")
    rows, (depth, units) = inputs.shape[0], w_gate.shape
    count = 4 * rows
    in_line = line(columns(inputs, depth).reshape(count, depth))
    cot_line = line(columns(grad_out, depth).reshape(count, depth))
    weights = (w_gate, w_up, w_down)
    grads, projected = [], []
    halves = []
    total = None

    def spread_back(k):
        part = back(grads[k][0], grads[k][1], w_gate, w_up)
        if k == 0:
            return part
        return swap(part.astype(bf16), k, "tensor").astype(f32)

    total = None
    for k in range(4):
        x, g = in_line[k], cot_line[k]
        if k == 1:
            x, g = after(x, *halves[0]), after(g, *halves[0])
        elif k > 1:
            x, g = after(x, grads[k - 2][0]), after(g, grads[k - 2][0])
        halves.append([halved(part) for part in partials(x, g, *weights)])
        hidden, gate_grad, upper_grad = middle(*[finished(half) for half in halves[k]])
        grads.append((gate_grad, upper_grad))
        projected.append(project(hidden, gate_grad, upper_grad, proj_gate, proj_up, proj_hidden))
    for k in range(4):
        part = spread_back(k)
        total = part if total is None else total + part
    d_input = uncolumns(total.astype(bf16).reshape(4, rows, depth))

    own = jnp.stack(
        [
            jnp.dot(inputs, proj_input, preferred_element_type=f32),
            jnp.dot(grad_out, proj_out, preferred_element_type=f32),
        ]
    )
    here = (jnp.arange(4) == me)[None, :, None, None]
    parts = jnp.take(jnp.stack(projected, axis=1), jnp.arange(4) ^ me, axis=1)
    parts = jnp.concatenate([parts, jnp.where(here, own[:, None], 0.0)])
    parts = parts + swap(parts, 1, "tensor")
    parts = parts + swap(parts, 2, "tensor")
    return d_input, parts.reshape(5, count, R)


def general(inputs, grad_out, w_gate, w_up, w_down, proj_input, proj_gate, proj_up, proj_hidden, proj_out):
    tensor_size = lax.axis_size("tensor")
    rows, (depth, units) = inputs.shape[0], w_gate.shape
    parts = min(PARTS, rows)
    step = rows // parts
    tokens = tensor_size * step
    in_cols, cot_cols = columns(inputs, depth), columns(grad_out, depth)
    own = jnp.stack(
        [
            jnp.dot(inputs, proj_input, preferred_element_type=f32),
            jnp.dot(grad_out, proj_out, preferred_element_type=f32),
        ]
    )
    own = lax.all_gather(own, "tensor", axis=1, tiled=True)

    def gathered(value, k):
        full = lax.all_gather(value[:, k * step : (k + 1) * step], "tensor", axis=1, tiled=True)
        return full.reshape(4 * tokens, depth)

    projected, returned = [], []
    for k in range(parts):
        sums = partials(gathered(in_cols, k), gathered(cot_cols, k), w_gate, w_up, w_down)
        hidden, gate_grad, upper_grad = middle(*[finished(halved(part)) for part in sums])
        part = project(hidden, gate_grad, upper_grad, proj_gate, proj_up, proj_hidden)
        projected.append(part.reshape(3, tensor_size, step, R))
        d_part = back(gate_grad, upper_grad, w_gate, w_up).reshape(4, tokens, depth)
        d_own = lax.psum_scatter(d_part, "tensor", scatter_dimension=1, tiled=True)
        returned.append(d_own.astype(bf16))
    d_input = uncolumns(jnp.concatenate(returned, axis=1))
    projections = jnp.stack(projected, axis=2).reshape(3, tensor_size * rows, R)
    return d_input, jnp.concatenate([lax.psum(projections, "tensor"), own])


def per_device(*args):
    example_ids = args[-1]
    dp_size, tensor_size = lax.axis_size("dp"), lax.axis_size("tensor")
    d_input, projections = (four if tensor_size == 4 else general)(*args[:-1])
    gate_proj, up_proj, hidden_proj, input_proj, out_proj = projections
    local_ids = example_ids[0]
    numbers = lax.broadcasted_iota(jnp.int32, (EX_DP, local_ids.shape[0]), 0)
    onehot = (local_ids[None, :] == numbers).astype(f32)
    stacked = jnp.stack(
        [
            example_grads(onehot, input_proj, gate_proj),
            example_grads(onehot, input_proj, up_proj),
            example_grads(onehot, hidden_proj, out_proj),
        ]
    )
    grads = stacked.reshape(3, EX_DP, R * R)
    left_side = jnp.einsum("meik,mejk->mij", stacked, stacked, precision=lax.Precision.HIGHEST)
    right_side = jnp.einsum("meki,mekj->mij", stacked, stacked, precision=lax.Precision.HIGHEST)
    total = jnp.stack([left_side, right_side], axis=1)
    total = total + swap(total, 1)
    total = total + swap(total, 2)
    fisher = (total / (EX_DP * dp_size)).reshape(3, 2, R * R)
    return (d_input, grads, fisher)


def solution(mesh):
    return jax.shard_map(
        per_device,
        mesh=mesh,
        in_specs=(
            P(("groups", "dp", "tensor"), None),
            P(("groups", "dp", "tensor"), None),
            P("dp", "tensor"),
            P("dp", "tensor"),
            P("tensor", "dp"),
            P(),
            P("tensor", None),
            P("tensor", None),
            P("tensor", None),
            P(),
            P(("groups", "dp"), None),
        ),
        out_specs=(
            P(("groups", "dp", "tensor"), None),
            P(None, ("groups", "dp"), None),
            P("groups", None, None),
        ),
        check_vma=False,
    )
```

```python
import jax
import jax.numpy as jnp
from jax import lax
from jax.experimental import pallas as pl
from jax.experimental.pallas import tpu as pltpu
from jax.sharding import PartitionSpec as P

R = 32
EX_DP = 4
PARTS = 2
ORDER = (0, 2, 1, 3)
CONTRACT = (((1,), (1,)), ((), ()))
f32, bf16 = jnp.float32, jnp.bfloat16


def example_grads(onehot, left, right):
    return 0.125 * jnp.einsum("et,ti,tj->eij", onehot, left, right, precision=lax.Precision.HIGHEST)


def swap(value, bit, axis="dp"):
    return lax.ppermute(value, axis, [(i, i ^ bit) for i in range(lax.axis_size(axis))])


def after(value, *others):
    return lax.optimization_barrier((value,) + others)[0]


def columns(value, depth):
    me = lax.axis_index("dp")
    slots = []
    for b in ORDER:
        block = lax.dynamic_slice_in_dim(value, (me ^ b) * depth, depth, value.ndim - 1)
        slots.append(block if b == 0 else swap(block, b))
    return jnp.stack(slots, axis=value.ndim - 2)


def uncolumns(slots):
    me = lax.axis_index("dp")
    count, rows, depth = slots.shape
    came = [slots[at] if b == 0 else swap(slots[at], b) for at, b in enumerate(ORDER)]
    where = jnp.array([ORDER.index(b) for b in range(count)], jnp.int32)[jnp.arange(count) ^ me]
    return jnp.take(jnp.stack(came), where, axis=0).transpose(1, 0, 2).reshape(rows, count * depth)


def halved(part):
    part = part.reshape(2, part.shape[0] // 2, part.shape[1])
    return part[0] + swap(part[1], 1)


def finished(half):
    half = half.reshape(2, half.shape[0] // 2, half.shape[1])
    return half[0] + swap(half[1].astype(bf16), 2).astype(f32)


def spread(value):
    pair = jnp.concatenate([value, swap(value, 2)])
    return jnp.concatenate([pair, swap(pair, 1)])


def partials(x, g, w_gate, w_up, w_down):
    return (
        jnp.dot(x, w_gate, preferred_element_type=f32),
        jnp.dot(x, w_up, preferred_element_type=f32),
        lax.dot_general(g, w_down, CONTRACT, preferred_element_type=f32),
    )


def middle(gate, upper, hidden_grad):
    sigma = jax.nn.sigmoid(gate)
    active = gate * sigma
    hidden = (active * upper).astype(bf16)
    upper_grad = (hidden_grad * active).astype(bf16)
    gate_grad = (hidden_grad * upper * sigma * (1.0 + gate * (1.0 - sigma))).astype(bf16)
    return hidden, gate_grad, upper_grad


def project(hidden, gate_grad, upper_grad, proj_gate, proj_up, proj_hidden):
    return jnp.stack(
        [
            jnp.dot(gate_grad, proj_gate, preferred_element_type=f32),
            jnp.dot(upper_grad, proj_up, preferred_element_type=f32),
            jnp.dot(hidden, proj_hidden, preferred_element_type=f32),
        ]
    )


def back(gate_grad, upper_grad, w_gate, w_up):
    part = lax.dot_general(spread(gate_grad), w_gate, CONTRACT, preferred_element_type=f32)
    return part + lax.dot_general(spread(upper_grad), w_up, CONTRACT, preferred_element_type=f32)


def line(own):
    me = lax.axis_index("tensor")
    left = [own]
    right = [own]
    for s in range(1, 4):
        left.append(lax.ppermute(left[-1], "tensor", [(t, t + 1) for t in range(s - 1, 3)]))
        right.append(lax.ppermute(right[-1], "tensor", [(t + 1, t) for t in range(0, 4 - s)]))
    second = jnp.where(me % 2 == 0, right[1], left[1])
    third = jnp.where(me < 2, right[2], left[2])
    near = jnp.where(me == 1, right[1], left[1])
    far = jnp.where(me == 0, right[3], left[3])
    return own, second, third, jnp.where((me == 0) | (me == 3), far, near)


def params():
    return pltpu.CompilerParams(vmem_limit_bytes=40 * 2**20, dimension_semantics=("arbitrary",))


def forward_kernel(x_ref, gate_ref, up_ref, down_ref, keep_ref, send_ref):
    half = x_ref.shape[1] // 2
    parts = partials(x_ref[0], x_ref[1], gate_ref[...], up_ref[...], down_ref[...])
    for n, part in enumerate(parts):
        keep_ref[n] = part[:half]
        send_ref[n] = part[half:]


def forward(x, w_gate, w_up, w_down, tile):
    _, tokens, depth = x.shape
    units = w_gate.shape[1]
    out = jax.ShapeDtypeStruct((3, tokens // 2, units), f32)
    spec = pl.BlockSpec((3, tokens // 2, tile), lambda n: (0, 0, n))
    return pl.pallas_call(
        forward_kernel,
        grid=(units // tile,),
        in_specs=[
            pl.BlockSpec((2, tokens, depth), lambda n: (0, 0, 0)),
            pl.BlockSpec((depth, tile), lambda n: (0, n)),
            pl.BlockSpec((depth, tile), lambda n: (0, n)),
            pl.BlockSpec((tile, depth), lambda n: (n, 0)),
        ],
        out_specs=[spec, spec],
        out_shape=[out, out],
        compiler_params=params(),
        cost_estimate=pl.CostEstimate(
            flops=6 * tokens * depth * units, bytes_accessed=6 * depth * units, transcendentals=0
        ),
    )(x, w_gate, w_up, w_down)


def middle_kernel(keep_ref, core_ref, chip_ref, pg_ref, pu_ref, ph_ref, grad_ref, proj_ref):
    sums = [keep_ref[n] + core_ref[n] + chip_ref[n].astype(f32) for n in range(3)]
    hidden, gate_grad, upper_grad = middle(*sums)
    grad_ref[0] = gate_grad
    grad_ref[1] = upper_grad

    @pl.when(pl.program_id(0) == 0)
    def _():
        proj_ref[...] = jnp.zeros_like(proj_ref)

    for n, (value, ref) in enumerate(((gate_grad, pg_ref), (upper_grad, pu_ref), (hidden, ph_ref))):
        proj_ref[n] += jnp.dot(value, ref[...], preferred_element_type=f32)


def middle_call(keep, core, chip, proj_gate, proj_up, proj_hidden, tile):
    _, rows, units = chip.shape
    spec = pl.BlockSpec((3, rows, tile), lambda n: (0, 0, n))
    proj = pl.BlockSpec((tile, R), lambda n: (n, 0))
    return pl.pallas_call(
        middle_kernel,
        grid=(units // tile,),
        in_specs=[spec, spec, spec, proj, proj, proj],
        out_specs=[
            pl.BlockSpec((2, rows, tile), lambda n: (0, 0, n)),
            pl.BlockSpec((3, rows, R), lambda n: (0, 0, 0)),
        ],
        out_shape=[
            jax.ShapeDtypeStruct((2, rows, units), bf16),
            jax.ShapeDtypeStruct((3, rows, R), f32),
        ],
        compiler_params=params(),
        cost_estimate=pl.CostEstimate(
            flops=40 * rows * units, bytes_accessed=34 * rows * units, transcendentals=rows * units
        ),
    )(keep, core, chip, proj_gate, proj_up, proj_hidden)


def back_kernel(a_ref, b_ref, c_ref, d_ref, gate_ref, up_ref, out_ref, grads):
    rows = a_ref.shape[1]

    @pl.when(pl.program_id(0) == 0)
    def _():
        for at, ref in enumerate((a_ref, b_ref, c_ref, d_ref)):
            grads[:, at * rows : (at + 1) * rows] = ref[...]

    part = lax.dot_general(grads[0], gate_ref[...], CONTRACT, preferred_element_type=f32)
    part += lax.dot_general(grads[1], up_ref[...], CONTRACT, preferred_element_type=f32)
    out_ref[...] = part.astype(out_ref.dtype)


def back_call(slots, w_gate, w_up, tile, dtype):
    _, rows, units = slots[0].shape
    depth, tokens = w_gate.shape[0], 4 * rows
    spec = pl.BlockSpec((2, rows, units), lambda n: (0, 0, 0))
    weight = pl.BlockSpec((tile, units), lambda n: (n, 0))
    return pl.pallas_call(
        back_kernel,
        grid=(depth // tile,),
        in_specs=[spec] * 4 + [weight, weight],
        out_specs=pl.BlockSpec((tokens, tile), lambda n: (0, n)),
        out_shape=jax.ShapeDtypeStruct((tokens, depth), dtype),
        scratch_shapes=[pltpu.VMEM((2, tokens, units), bf16)],
        compiler_params=params(),
        cost_estimate=pl.CostEstimate(
            flops=4 * tokens * depth * units, bytes_accessed=4 * depth * units, transcendentals=0
        ),
    )(*slots, w_gate, w_up)


def four(inputs, grad_out, w_gate, w_up, w_down, proj_input, proj_gate, proj_up, proj_hidden, proj_out):
    me = lax.axis_index("tensor")
    rows, (depth, units) = inputs.shape[0], w_gate.shape
    count = 4 * rows
    both = columns(jnp.stack([inputs, grad_out]), depth)
    chunks = line(both.reshape(2, count, depth))
    halves, grads, projected = [], [], []
    total = None
    for k in range(4):
        x = chunks[k]
        if k == 1:
            x = after(x, halves[0])
        elif k > 1:
            x = after(x, grads[k - 2])
        keep, send = forward(x, w_gate, w_up, w_down, units // 7)
        core = swap(send, 1)
        halves.append((keep[:, rows:] + core[:, rows:]).astype(bf16))
        chip = swap(halves[k], 2)
        own, proj = middle_call(keep, core, chip, proj_gate, proj_up, proj_hidden, units // 4)
        grads.append(own)
        projected.append(proj)
        other = swap(own, 2)
        slots = [own, other, swap(own, 1), swap(other, 1)]
        part = back_call(slots, w_gate, w_up, depth // 8, f32 if k == 0 else bf16)
        if k == 0:
            total = part
        else:
            total = total + swap(part, k, "tensor").astype(f32)
    d_input = uncolumns(total.astype(bf16).reshape(4, rows, depth))

    own = jnp.stack(
        [
            jnp.dot(inputs, proj_input, preferred_element_type=f32),
            jnp.dot(grad_out, proj_out, preferred_element_type=f32),
        ]
    )
    here = (jnp.arange(4) == me)[None, :, None, None]
    parts = jnp.take(jnp.stack(projected, axis=1), jnp.arange(4) ^ me, axis=1)
    parts = jnp.concatenate([parts, jnp.where(here, own[:, None], 0.0)])
    parts = parts + swap(parts, 1, "tensor")
    parts = parts + swap(parts, 2, "tensor")
    return d_input, parts.reshape(5, count, R)


def general(inputs, grad_out, w_gate, w_up, w_down, proj_input, proj_gate, proj_up, proj_hidden, proj_out):
    tensor_size = lax.axis_size("tensor")
    rows, (depth, units) = inputs.shape[0], w_gate.shape
    parts = min(PARTS, rows)
    step = rows // parts
    tokens = tensor_size * step
    in_cols, cot_cols = columns(inputs, depth), columns(grad_out, depth)
    own = jnp.stack(
        [
            jnp.dot(inputs, proj_input, preferred_element_type=f32),
            jnp.dot(grad_out, proj_out, preferred_element_type=f32),
        ]
    )
    own = lax.all_gather(own, "tensor", axis=1, tiled=True)

    def gathered(value, k):
        full = lax.all_gather(value[:, k * step : (k + 1) * step], "tensor", axis=1, tiled=True)
        return full.reshape(4 * tokens, depth)

    projected, returned = [], []
    for k in range(parts):
        sums = partials(gathered(in_cols, k), gathered(cot_cols, k), w_gate, w_up, w_down)
        hidden, gate_grad, upper_grad = middle(*[finished(halved(part)) for part in sums])
        part = project(hidden, gate_grad, upper_grad, proj_gate, proj_up, proj_hidden)
        projected.append(part.reshape(3, tensor_size, step, R))
        d_part = back(gate_grad, upper_grad, w_gate, w_up).reshape(4, tokens, depth)
        d_own = lax.psum_scatter(d_part, "tensor", scatter_dimension=1, tiled=True)
        returned.append(d_own.astype(bf16))
    d_input = uncolumns(jnp.concatenate(returned, axis=1))
    projections = jnp.stack(projected, axis=2).reshape(3, tensor_size * rows, R)
    return d_input, jnp.concatenate([lax.psum(projections, "tensor"), own])


def per_device(*args):
    example_ids = args[-1]
    dp_size, tensor_size = lax.axis_size("dp"), lax.axis_size("tensor")
    d_input, projections = (four if tensor_size == 4 else general)(*args[:-1])
    gate_proj, up_proj, hidden_proj, input_proj, out_proj = projections
    local_ids = example_ids[0]
    numbers = lax.broadcasted_iota(jnp.int32, (EX_DP, local_ids.shape[0]), 0)
    onehot = (local_ids[None, :] == numbers).astype(f32)
    stacked = jnp.stack(
        [
            example_grads(onehot, input_proj, gate_proj),
            example_grads(onehot, input_proj, up_proj),
            example_grads(onehot, hidden_proj, out_proj),
        ]
    )
    grads = stacked.reshape(3, EX_DP, R * R)
    left_side = jnp.einsum("meik,mejk->mij", stacked, stacked, precision=lax.Precision.HIGHEST)
    right_side = jnp.einsum("meki,mekj->mij", stacked, stacked, precision=lax.Precision.HIGHEST)
    total = jnp.stack([left_side, right_side], axis=1)
    total = total + swap(total, 1)
    total = total + swap(total, 2)
    fisher = (total / (EX_DP * dp_size)).reshape(3, 2, R * R)
    return (d_input, grads, fisher)


def solution(mesh):
    return jax.shard_map(
        per_device,
        mesh=mesh,
        in_specs=(
            P(("groups", "dp", "tensor"), None),
            P(("groups", "dp", "tensor"), None),
            P("dp", "tensor"),
            P("dp", "tensor"),
            P("tensor", "dp"),
            P(),
            P("tensor", None),
            P("tensor", None),
            P("tensor", None),
            P(),
            P(("groups", "dp"), None),
        ),
        out_specs=(
            P(("groups", "dp", "tensor"), None),
            P(None, ("groups", "dp"), None),
            P("groups", None, None),
        ),
        check_vma=False,
    )
```

```python
import jax
import jax.numpy as jnp
from jax import lax
from jax.experimental import pallas as pl
from jax.experimental.pallas import tpu as pltpu
from jax.sharding import PartitionSpec as P

R = 32
EX_DP = 4
PARTS = 2
ORDER = (0, 2, 1, 3)
GROUPS = ((0,), (1,), (2,), (3,))
CONTRACT = (((1,), (1,)), ((), ()))
f32, bf16 = jnp.float32, jnp.bfloat16


def example_grads(onehot, left, right):
    return 0.125 * jnp.einsum("et,ti,tj->eij", onehot, left, right, precision=lax.Precision.HIGHEST)


def swap(value, bit, axis="dp"):
    return lax.ppermute(value, axis, [(i, i ^ bit) for i in range(lax.axis_size(axis))])


def after(value, *others):
    return lax.optimization_barrier((value,) + others)[0]


def columns(value, depth):
    me = lax.axis_index("dp")
    slots = []
    for b in ORDER:
        block = lax.dynamic_slice_in_dim(value, (me ^ b) * depth, depth, value.ndim - 1)
        slots.append(block if b == 0 else swap(block, b))
    return jnp.stack(slots, axis=value.ndim - 2)


def uncolumns(slots):
    me = lax.axis_index("dp")
    count, rows, depth = slots.shape
    came = [slots[at] if b == 0 else swap(slots[at], b) for at, b in enumerate(ORDER)]
    where = jnp.array([ORDER.index(b) for b in range(count)], jnp.int32)[jnp.arange(count) ^ me]
    return jnp.take(jnp.stack(came), where, axis=0).transpose(1, 0, 2).reshape(rows, count * depth)


def halved(part):
    part = part.reshape(2, part.shape[0] // 2, part.shape[1])
    return part[0] + swap(part[1], 1)


def finished(half):
    half = half.reshape(2, half.shape[0] // 2, half.shape[1])
    return half[0] + swap(half[1].astype(bf16), 2).astype(f32)


def spread(value):
    pair = jnp.concatenate([value, swap(value, 2)])
    return jnp.concatenate([pair, swap(pair, 1)])


def partials(x, g, w_gate, w_up, w_down):
    return (
        jnp.dot(x, w_gate, preferred_element_type=f32),
        jnp.dot(x, w_up, preferred_element_type=f32),
        lax.dot_general(g, w_down, CONTRACT, preferred_element_type=f32),
    )


def middle(gate, upper, hidden_grad):
    sigma = jax.nn.sigmoid(gate)
    active = gate * sigma
    hidden = (active * upper).astype(bf16)
    upper_grad = (hidden_grad * active).astype(bf16)
    gate_grad = (hidden_grad * upper * sigma * (1.0 + gate * (1.0 - sigma))).astype(bf16)
    return hidden, gate_grad, upper_grad


def project(hidden, gate_grad, upper_grad, proj_gate, proj_up, proj_hidden):
    return jnp.stack(
        [
            jnp.dot(gate_grad, proj_gate, preferred_element_type=f32),
            jnp.dot(upper_grad, proj_up, preferred_element_type=f32),
            jnp.dot(hidden, proj_hidden, preferred_element_type=f32),
        ]
    )


def back(gate_grad, upper_grad, w_gate, w_up):
    part = lax.dot_general(spread(gate_grad), w_gate, CONTRACT, preferred_element_type=f32)
    return part + lax.dot_general(spread(upper_grad), w_up, CONTRACT, preferred_element_type=f32)


def hop(left, right, s):
    left.append(lax.ppermute(left[-1], "tensor", [(t, t + 1) for t in range(s - 1, 3)]))
    right.append(lax.ppermute(right[-1], "tensor", [(t + 1, t) for t in range(0, 4 - s)]))


def chosen(left, right, s):
    me = lax.axis_index("tensor")
    if s == 0:
        return left[0]
    if s == 1:
        return jnp.where(me % 2 == 0, right[1], left[1])
    if s == 2:
        return jnp.where(me < 2, right[2], left[2])
    near = jnp.where(me == 1, right[1], left[1])
    far = jnp.where(me == 0, right[3], left[3])
    return jnp.where((me == 0) | (me == 3), far, near)


def params():
    return pltpu.CompilerParams(vmem_limit_bytes=40 * 2**20, dimension_semantics=("arbitrary",))


def forward_kernel(x_ref, gate_ref, up_ref, down_ref, keep_ref, send_ref):
    half = x_ref.shape[1] // 2
    parts = partials(x_ref[0], x_ref[1], gate_ref[...], up_ref[...], down_ref[...])
    for n, part in enumerate(parts):
        keep_ref[n] = part[:half]
        send_ref[n] = part[half:]


def forward(x, w_gate, w_up, w_down, tile):
    _, tokens, depth = x.shape
    units = w_gate.shape[1]
    out = jax.ShapeDtypeStruct((3, tokens // 2, units), f32)
    spec = pl.BlockSpec((3, tokens // 2, tile), lambda n: (0, 0, n))
    return pl.pallas_call(
        forward_kernel,
        grid=(units // tile,),
        in_specs=[
            pl.BlockSpec((2, tokens, depth), lambda n: (0, 0, 0)),
            pl.BlockSpec((depth, tile), lambda n: (0, n)),
            pl.BlockSpec((depth, tile), lambda n: (0, n)),
            pl.BlockSpec((tile, depth), lambda n: (n, 0)),
        ],
        out_specs=[spec, spec],
        out_shape=[out, out],
        compiler_params=params(),
        cost_estimate=pl.CostEstimate(
            flops=6 * tokens * depth * units, bytes_accessed=6 * depth * units, transcendentals=0
        ),
    )(x, w_gate, w_up, w_down)


def middle_kernel(keep_ref, core_ref, chip_ref, pg_ref, pu_ref, ph_ref, grad_ref, proj_ref):
    sums = [keep_ref[n] + core_ref[n] + chip_ref[n].astype(f32) for n in range(3)]
    hidden, gate_grad, upper_grad = middle(*sums)
    grad_ref[0] = gate_grad
    grad_ref[1] = upper_grad

    @pl.when(pl.program_id(0) == 0)
    def _():
        proj_ref[...] = jnp.zeros_like(proj_ref)

    for n, (value, ref) in enumerate(((gate_grad, pg_ref), (upper_grad, pu_ref), (hidden, ph_ref))):
        proj_ref[n] += jnp.dot(value, ref[...], preferred_element_type=f32)


def middle_call(keep, core, chip, proj_gate, proj_up, proj_hidden, tile):
    _, rows, units = chip.shape
    spec = pl.BlockSpec((3, rows, tile), lambda n: (0, 0, n))
    proj = pl.BlockSpec((tile, R), lambda n: (n, 0))
    return pl.pallas_call(
        middle_kernel,
        grid=(units // tile,),
        in_specs=[spec, spec, spec, proj, proj, proj],
        out_specs=[
            pl.BlockSpec((2, rows, tile), lambda n: (0, 0, n)),
            pl.BlockSpec((3, rows, R), lambda n: (0, 0, 0)),
        ],
        out_shape=[
            jax.ShapeDtypeStruct((2, rows, units), bf16),
            jax.ShapeDtypeStruct((3, rows, R), f32),
        ],
        compiler_params=params(),
        cost_estimate=pl.CostEstimate(
            flops=40 * rows * units, bytes_accessed=34 * rows * units, transcendentals=rows * units
        ),
    )(keep, core, chip, proj_gate, proj_up, proj_hidden)


def back_kernel(a_ref, b_ref, c_ref, d_ref, gate_ref, up_ref, out_ref, grads):
    rows = a_ref.shape[1]

    @pl.when(pl.program_id(0) == 0)
    def _():
        for at, ref in enumerate((a_ref, b_ref, c_ref, d_ref)):
            grads[:, at * rows : (at + 1) * rows] = ref[...]

    part = lax.dot_general(grads[0], gate_ref[...], CONTRACT, preferred_element_type=f32)
    part += lax.dot_general(grads[1], up_ref[...], CONTRACT, preferred_element_type=f32)
    out_ref[...] = part.astype(out_ref.dtype)


def back_call(slots, w_gate, w_up, tile, dtype):
    _, rows, units = slots[0].shape
    depth, tokens = w_gate.shape[0], 4 * rows
    spec = pl.BlockSpec((2, rows, units), lambda n: (0, 0, 0))
    weight = pl.BlockSpec((tile, units), lambda n: (n, 0))
    return pl.pallas_call(
        back_kernel,
        grid=(depth // tile,),
        in_specs=[spec] * 4 + [weight, weight],
        out_specs=pl.BlockSpec((tokens, tile), lambda n: (0, n)),
        out_shape=jax.ShapeDtypeStruct((tokens, depth), dtype),
        scratch_shapes=[pltpu.VMEM((2, tokens, units), bf16)],
        compiler_params=params(),
        cost_estimate=pl.CostEstimate(
            flops=4 * tokens * depth * units, bytes_accessed=4 * depth * units, transcendentals=0
        ),
    )(*slots, w_gate, w_up)


def four(inputs, grad_out, w_gate, w_up, w_down, proj_input, proj_gate, proj_up, proj_hidden, proj_out):
    me = lax.axis_index("tensor")
    rows, (depth, units) = inputs.shape[0], w_gate.shape
    count = 4 * rows
    both = columns(jnp.stack([inputs, grad_out]), depth)
    left = [both.reshape(2, count, depth)]
    right = [left[0]]
    halves, grads, projected = [], [], [None] * 4
    total = 0.0
    parts = []
    done = 0
    for k, group in enumerate(GROUPS):
        while done < group[-1]:
            done += 1
            if done > 1 and halves:
                last = halves[min(done - 2, len(halves) - 1)]
                left[-1], right[-1] = lax.optimization_barrier((left[-1], right[-1], last))[:2]
            hop(left, right, done)
        wide = len(group) * rows
        x = [chosen(left, right, s).reshape(2, 4, rows, depth) for s in group]
        x = jnp.concatenate(x, axis=2).reshape(2, 4 * wide, depth)
        if k == 1:
            x = after(x, halves[0])
        elif k > 1:
            x = after(x, grads[k - 2], *parts[: k - 2])
        keep, send = forward(x, w_gate, w_up, w_down, units // 7)
        core = swap(send, 1)
        halves.append((keep[:, wide:] + core[:, wide:]).astype(bf16))
        chip = swap(halves[k], 2)
        if k > 2:
            chip = after(chip, parts[k - 2])
        own, proj = middle_call(keep, core, chip, proj_gate, proj_up, proj_hidden, units // 4)
        grads.append(own)
        other = swap(own, 2)
        slots = [own, other, swap(own, 1), swap(other, 1)]
        part = back_call(slots, w_gate, w_up, depth // 8, f32 if 0 in group else bf16)
        parts.append(part)
        part = part.reshape(4, len(group), rows, depth)
        for at, s in enumerate(group):
            projected[s] = proj[:, at * rows : (at + 1) * rows]
            one = part[:, at]
            total = total + (one if s == 0 else swap(one.astype(bf16), s, "tensor").astype(f32))
    d_input = uncolumns(total.astype(bf16))

    own = jnp.stack(
        [
            jnp.dot(inputs, proj_input, preferred_element_type=f32),
            jnp.dot(grad_out, proj_out, preferred_element_type=f32),
        ]
    )
    here = (jnp.arange(4) == me)[None, :, None, None]
    parts = jnp.take(jnp.stack(projected, axis=1), jnp.arange(4) ^ me, axis=1)
    parts = jnp.concatenate([parts, jnp.where(here, own[:, None], 0.0)])
    parts = parts + swap(parts, 1, "tensor")
    parts = parts + swap(parts, 2, "tensor")
    return d_input, parts.reshape(5, count, R)


def general(inputs, grad_out, w_gate, w_up, w_down, proj_input, proj_gate, proj_up, proj_hidden, proj_out):
    tensor_size = lax.axis_size("tensor")
    rows, (depth, units) = inputs.shape[0], w_gate.shape
    parts = min(PARTS, rows)
    step = rows // parts
    tokens = tensor_size * step
    in_cols, cot_cols = columns(inputs, depth), columns(grad_out, depth)
    own = jnp.stack(
        [
            jnp.dot(inputs, proj_input, preferred_element_type=f32),
            jnp.dot(grad_out, proj_out, preferred_element_type=f32),
        ]
    )
    own = lax.all_gather(own, "tensor", axis=1, tiled=True)

    def gathered(value, k):
        full = lax.all_gather(value[:, k * step : (k + 1) * step], "tensor", axis=1, tiled=True)
        return full.reshape(4 * tokens, depth)

    projected, returned = [], []
    for k in range(parts):
        sums = partials(gathered(in_cols, k), gathered(cot_cols, k), w_gate, w_up, w_down)
        hidden, gate_grad, upper_grad = middle(*[finished(halved(part)) for part in sums])
        part = project(hidden, gate_grad, upper_grad, proj_gate, proj_up, proj_hidden)
        projected.append(part.reshape(3, tensor_size, step, R))
        d_part = back(gate_grad, upper_grad, w_gate, w_up).reshape(4, tokens, depth)
        d_own = lax.psum_scatter(d_part, "tensor", scatter_dimension=1, tiled=True)
        returned.append(d_own.astype(bf16))
    d_input = uncolumns(jnp.concatenate(returned, axis=1))
    projections = jnp.stack(projected, axis=2).reshape(3, tensor_size * rows, R)
    return d_input, jnp.concatenate([lax.psum(projections, "tensor"), own])


def per_device(*args):
    example_ids = args[-1]
    dp_size, tensor_size = lax.axis_size("dp"), lax.axis_size("tensor")
    d_input, projections = (four if tensor_size == 4 else general)(*args[:-1])
    gate_proj, up_proj, hidden_proj, input_proj, out_proj = projections
    local_ids = example_ids[0]
    numbers = lax.broadcasted_iota(jnp.int32, (EX_DP, local_ids.shape[0]), 0)
    onehot = (local_ids[None, :] == numbers).astype(f32)
    stacked = jnp.stack(
        [
            example_grads(onehot, input_proj, gate_proj),
            example_grads(onehot, input_proj, up_proj),
            example_grads(onehot, hidden_proj, out_proj),
        ]
    )
    grads = stacked.reshape(3, EX_DP, R * R)
    left_side = jnp.einsum("meik,mejk->mij", stacked, stacked, precision=lax.Precision.HIGHEST)
    right_side = jnp.einsum("meki,mekj->mij", stacked, stacked, precision=lax.Precision.HIGHEST)
    total = jnp.stack([left_side, right_side], axis=1)
    total = total + swap(total, 1)
    total = total + swap(total, 2)
    fisher = (total / (EX_DP * dp_size)).reshape(3, 2, R * R)
    return (d_input, grads, fisher)


def solution(mesh):
    return jax.shard_map(
        per_device,
        mesh=mesh,
        in_specs=(
            P(("groups", "dp", "tensor"), None),
            P(("groups", "dp", "tensor"), None),
            P("dp", "tensor"),
            P("dp", "tensor"),
            P("tensor", "dp"),
            P(),
            P("tensor", None),
            P("tensor", None),
            P("tensor", None),
            P(),
            P(("groups", "dp"), None),
        ),
        out_specs=(
            P(("groups", "dp", "tensor"), None),
            P(None, ("groups", "dp"), None),
            P("groups", None, None),
        ),
        check_vma=False,
    )
```
